32 devices in a mesh: groups: 2 (over x), lon: 8 (over z, y), ens: 2 (over core).
Axes of the slice: x: 2, y: 2, z: 4, core: 2. Of those that a mesh axis runs over, the one named last changes fastest.
Arguments:
- inputs: bfloat16 [8, 16, 512, 512], P('ens', 'groups', 'lon'), parts along dimension 1, may hold values from -6 to 6
- layer_norm_gain: float32 [512], replicated, may hold values from 0.5 to 1.5
- w_qkv: bfloat16 [512, 1536], replicated, as said below
- w_out: bfloat16 [512, 512], replicated, may hold values from -0.25 to 0.25
- w_head: bfloat16 [512, 128], replicated, may hold values from -0.25 to 0.25
- target: float32 [16, 512, 128], P('groups', 'lon'), parts along dimension 0, may hold values from -6 to 6
Outputs:
- grad_input: bfloat16 [8, 16, 512, 512], P('ens', 'groups', 'lon'), parts along dimension 1
- grad_qkv: float32 [1024, 1536], P(('groups', 'lon')), parts along dimension 0
- grad_out: float32 [1024, 512], P(('groups', 'lon')), parts along dimension 0
- grad_head: float32 [1024, 128], P(('groups', 'lon')), parts along dimension 0
The draws below stay inside these ranges and needn't reach their ends.
There are 2 independent parts, one for each index of `groups`. The reference program is written for one: setup_inputs(seed, part) draws one part's arguments, and reference() takes and returns one part's arrays. A program takes and returns all parts, laid end to end along the dimension named above; an argument that names none is the same for every part. Nothing has to cross between parts.
Inputs may be any that keep to these rules, and one draw needn't show every extreme that they name: `w_qkv`: entries are independent across rows and of order 512 ** -0.5 times a few.
All inputs are finite; a program needn't handle non-finite values.
Results may differ from the reference program's by a relative error of at most 0.019.
Values may be sent and summed in bfloat16 or wider, within the bound.
No kernel may reach another device: no remote copies, remote signals or barrier semaphores. Data moves between devices by JAX's collectives and lax.ppermute only.
A program may use at most 192 MiB of HBM per device.

```python
import math
import jax
import jax.numpy as jnp
from jax import lax

D = 512
HEADS = 16
VARS = 128
MEM = 8
LAT = 8
LON = 512


def draw_w_qkv(key, part):
    base = jax.random.normal(key, (D, 3 * D), jnp.float32) / math.sqrt(D)
    base = jnp.clip(base, -5.0 / math.sqrt(D), 5.0 / math.sqrt(D))
    return base.astype(jnp.bfloat16)


def block_levels(key, extent, pieces, low, high):
    gain = 1.0
    for position, shards_of in pieces:
        heights = jax.random.uniform(jax.random.fold_in(jax.random.fold_in(key, 6), position), (shards_of,), jnp.float32, low / len(pieces), high / len(pieces))
        gain = gain * jnp.repeat(jnp.exp(heights), extent[position] // shards_of).reshape((-1,) + (1,) * (len(extent) - 1 - position))
    return gain


def scatter_about(stream_key, shape, deviation, most, cuts=(), held_as=jnp.bfloat16):
    entries = jax.random.normal(stream_key, shape, jnp.float32) * deviation
    if len(cuts) > 0:
        entries = block_levels(stream_key, shape, cuts, -0.22, 0.18) * entries
    return jnp.clip(entries, min=-most, max=most).astype(held_as)


def setup_inputs(seed: int = 0, part: int = 0) -> dict:
    seeds = jax.random.split(jax.random.key(seed), 7)
    part_keys = jax.random.split(jax.random.fold_in(seeds[6], part), 7)
    inputs = scatter_about(part_keys[0], (MEM, LAT, LON, D), 1.0, 6.0, ((0, 2), (2, 8)))
    layer_norm_gain = jnp.clip(1.0 + 0.1 * jax.random.normal(seeds[1], (D,), jnp.float32), 0.5, 1.5)
    w_qkv = draw_w_qkv(jax.random.fold_in(seeds[6], 71), part)
    w_out = scatter_about(seeds[3], (D, D), D ** -0.5, 0.25)
    w_head = scatter_about(seeds[4], (D, VARS), D ** -0.5, 0.25)
    target = scatter_about(part_keys[5], (LAT, LON, VARS), 1.0, 6.0, ((1, 8),), jnp.float32)
    return {"inputs": inputs, "layer_norm_gain": layer_norm_gain, "w_qkv": w_qkv, "w_out": w_out, "w_head": w_head, "target": target}


eps_norm = 1e-05
smooth_width = 0.25
loss_scale = 32.0

def dot_t(left, right):
    return lax.dot_general(left, right, (((1,), (1,)), ((), ())), preferred_element_type=jnp.float32)

def dot_rows(left, right):
    return lax.dot_general(left, right, (((0,), (0,)), ((), ())), preferred_element_type=jnp.float32)

def slope(delta):
    return delta * lax.rsqrt(delta * delta + smooth_width * smooth_width)

def to_groups(field):
    members, lat, lon, chans = field.shape
    rows = lat // 8
    cols = lon // 8
    shaped = field.reshape(members, 8, rows, 8, cols, chans).transpose(0, 2, 4, 3, 1, 5)
    return shaped.reshape(members * rows * cols, 64, chans)

def from_groups(groups, members, lat, lon):
    rows = lat // 8
    cols = lon // 8
    chans = groups.shape[2]
    shaped = groups.reshape(members, rows, cols, 8, 8, chans).transpose(0, 4, 1, 3, 2, 5)
    return shaped.reshape(members, lat, lon, chans)

def heads_of(qkv):
    count, cells, three = qkv.shape
    width = three // 3
    parts = qkv.reshape(count, cells, 3, HEADS, width // HEADS).astype(jnp.float32)
    return (parts[:, :, 0], parts[:, :, 1], parts[:, :, 2])

def softmax_of(query, keys):
    scores = jnp.einsum('gqhd,gkhd->ghqk', query, keys) * query.shape[-1] ** (-0.5)
    top = lax.optimization_barrier(jnp.max(scores, axis=-1, keepdims=True))
    expo = jnp.exp(scores - top)
    return expo / lax.optimization_barrier(jnp.sum(expo, axis=-1, keepdims=True))

def attend(qkv):
    query, keys, values = heads_of(qkv)
    weights = softmax_of(query, keys).astype(jnp.bfloat16).astype(jnp.float32)
    out = jnp.einsum('ghqk,gkhd->gqhd', weights, values)
    return out.astype(jnp.bfloat16).reshape(qkv.shape[0], qkv.shape[1], -1)

def attend_back(pair):
    qkv, grad = pair
    query, keys, values = heads_of(qkv)
    probs = softmax_of(query, keys)
    weights = probs.astype(jnp.bfloat16).astype(jnp.float32)
    upstream = grad.astype(jnp.float32).reshape(query.shape)
    g_values = jnp.einsum('ghqk,gqhd->gkhd', weights, upstream).astype(jnp.bfloat16)
    g_probs = jnp.einsum('gqhd,gkhd->ghqk', upstream, values)
    inner = lax.optimization_barrier(jnp.sum(probs * g_probs, axis=-1, keepdims=True))
    g_scores = (probs * (g_probs - inner) * query.shape[-1] ** (-0.5)).astype(jnp.bfloat16).astype(jnp.float32)
    g_query = jnp.einsum('ghqk,gkhd->gqhd', g_scores, keys).astype(jnp.bfloat16)
    g_keys = jnp.einsum('ghqk,gqhd->gkhd', g_scores, query).astype(jnp.bfloat16)
    return jnp.stack([g_query, g_keys, g_values], axis=2).reshape(qkv.shape)

def reference(inputs, layer_norm_gain, w_qkv, w_out, w_head, target):
    members, lat, lon, width = inputs.shape
    input_float = inputs.astype(jnp.float32)
    feature_mean = lax.optimization_barrier(jnp.mean(input_float, axis=-1, keepdims=True))
    input_centered = input_float - feature_mean
    var = lax.optimization_barrier(jnp.mean(input_centered * input_centered, axis=-1, keepdims=True))
    inverse_deviation = lax.rsqrt(var + eps_norm)
    standardized_input = input_centered * inverse_deviation
    normed_input = (standardized_input * layer_norm_gain).astype(jnp.bfloat16)
    normed_flat = normed_input.reshape(-1, width)
    qkv = jnp.dot(normed_flat, w_qkv, preferred_element_type=jnp.float32).astype(jnp.bfloat16)
    groups = to_groups(qkv.reshape(members, lat, lon, 3 * width))
    count = groups.shape[0]
    blocks = groups.reshape(count // 8, 8, 64, 3 * width)
    attended_groups = lax.map(attend, blocks).reshape(count, 64, width)
    attended_flat = from_groups(attended_groups, members, lat, lon).reshape(-1, width)
    block_out = (input_float.reshape(-1, width) + jnp.dot(attended_flat, w_out, preferred_element_type=jnp.float32)).astype(jnp.bfloat16)
    pred = jnp.dot(block_out, w_head, preferred_element_type=jnp.float32).astype(jnp.bfloat16)
    predf = pred.astype(jnp.float32).reshape(members, lat, lon, -1)
    spread = jnp.zeros_like(predf)
    for other in range(members):
        spread = spread + slope(predf - predf[other])
    g_pred = (loss_scale / members * (slope(predf - target) - spread / (members - 1))).astype(jnp.bfloat16)
    g_pred_flat = g_pred.reshape(-1, g_pred.shape[-1])
    g_block = dot_t(g_pred_flat, w_head).astype(jnp.bfloat16)
    g_att = dot_t(g_block, w_out).astype(jnp.bfloat16)
    g_blocks = to_groups(g_att.reshape(members, lat, lon, width)).reshape(count // 8, 8, 64, width)
    g_qkv_groups = lax.map(attend_back, (blocks, g_blocks)).reshape(count, 64, 3 * width)
    g_qkv = from_groups(g_qkv_groups, members, lat, lon).reshape(-1, 3 * width)
    normed_input_gradient = dot_t(g_qkv, w_qkv).astype(jnp.bfloat16).reshape(members, lat, lon, width)
    scaled_input = normed_input_gradient.astype(jnp.float32) * layer_norm_gain
    norm_gradient = inverse_deviation * (scaled_input - lax.optimization_barrier(jnp.mean(scaled_input, axis=-1, keepdims=True)) - standardized_input * lax.optimization_barrier(jnp.mean(scaled_input * standardized_input, axis=-1, keepdims=True)))
    grad_input = (g_block.astype(jnp.float32).reshape(members, lat, lon, width) + norm_gradient).astype(jnp.bfloat16)
    grad_qkv = dot_rows(normed_flat, g_qkv)
    grad_out = dot_rows(attended_flat, g_block)
    grad_head = dot_rows(block_out, g_pred_flat)
    return (grad_input, grad_qkv, grad_out, grad_head)
```

```python
import functools

import jax
import jax.numpy as jnp
from jax import lax
from jax.experimental import pallas as pl
from jax.experimental.pallas import tpu as pltpu
from jax.sharding import Mesh
from jax.sharding import PartitionSpec as P

HEADS = 16
CELLS = 8
eps_norm = 1e-05
smooth_width = 0.25
loss_scale = 32.0
LOG2E = 1.4426950408889634
CHUNKS = 4

bf16 = jnp.bfloat16
f32 = jnp.float32


def dot(left, right):
    return jnp.dot(left, right, preferred_element_type=f32)


def dot_t(left, right):
    return lax.dot_general(left, right, (((1,), (1,)), ((), ())), preferred_element_type=f32)


def dot_rows(left, right):
    return lax.dot_general(left, right, (((0,), (0,)), ((), ())), preferred_element_type=f32)


def slope(delta):
    return delta * lax.rsqrt(delta * delta + smooth_width * smooth_width)


def expand(block, mask):
    return jnp.concatenate([block] * 4, axis=0) * mask


def diagonal(wide, lane, dim):
    cells = wide.shape[0] // 4
    out = wide[:cells]
    for h in range(1, 4):
        out = jnp.where(lane >= h * dim, wide[h * cells : (h + 1) * cells], out)
    return out


def block_kernel(members, width, chans, first, *refs):
    if first:
        x_ref, gain_ref, wqkv_ref, wout_ref, whead_ref, gx_ref, acc_ref = refs[:7]
        scratch = refs[7:]
        prev_ref = None
    else:
        x_ref, gain_ref, wqkv_ref, wout_ref, whead_ref, prev_ref, gx_ref, acc_ref = refs[:8]
        scratch = refs[8:]
    xf, normed, normed_t, qkv, g_qkv, att, probs, bout, g_pred, g_block, g_att, mask_ref, acc = scratch
    cells = CELLS * CELLS
    rows = members * cells
    half = members // 2
    dim = width // HEADS
    pack = 4 * dim
    packs = width // pack
    scale = dim ** (-0.5)
    step = pl.program_id(0)
    tile = 256

    @pl.when(step == 0)
    def _():
        if first:
            acc[...] = jnp.zeros_like(acc)
        else:
            acc[...] = prev_ref[...]
        row_head = lax.broadcasted_iota(jnp.int32, (4 * cells, pack), 0) // cells
        lane_head = lax.broadcasted_iota(jnp.int32, (4 * cells, pack), 1) // dim
        mask_ref[...] = jnp.where(row_head == lane_head, 1.0, 0.0).astype(bf16)

    lane = lax.broadcasted_iota(jnp.int32, (cells, pack), 1)

    for c in range(CELLS):
        for s in range(2):
            for m in range(half):
                top = (s * half + m) * cells + c * CELLS
                xf[top : top + CELLS, :] = x_ref[
                    c * 2 + s, 0, :, m * width : (m + 1) * width
                ].astype(f32)

    gain = gain_ref[...]

    @pl.loop(0, members)
    def _(m):
        at = pl.ds(pl.multiple_of(m * cells, cells), cells)
        x = xf[at, :]
        centered = x - jnp.mean(x, axis=-1, keepdims=True)
        var = jnp.mean(centered * centered, axis=-1, keepdims=True)
        normed[at, :] = (centered * lax.rsqrt(var + eps_norm) * gain).astype(bf16)

    @pl.loop(0, 3 * width // tile)
    def _(n):
        at = pl.ds(pl.multiple_of(n * tile, tile), tile)
        qkv[:, at] = dot(normed[...], wqkv_ref[:, at]).astype(bf16)

    @pl.loop(0, members)
    def _(m):
        at = pl.ds(pl.multiple_of(m * cells, cells), cells)
        mask = mask_ref[...]
        for p in range(packs):
            q = qkv[at, p * pack : (p + 1) * pack]
            k = qkv[at, width + p * pack : width + (p + 1) * pack]
            v = qkv[at, 2 * width + p * pack : 2 * width + (p + 1) * pack]
            scores = dot_t(k, expand(q, mask))
            top = jnp.max(scores, axis=0, keepdims=True)
            expo = jnp.exp2((scores - top) * (scale * LOG2E))
            prob = expo * (1.0 / jnp.sum(expo, axis=0, keepdims=True))
            probs[m, p] = prob
            out = dot_rows(prob.astype(bf16), v)
            att[at, p * pack : (p + 1) * pack] = diagonal(out, lane, dim).astype(bf16)

    bout[...] = (xf[...] + dot(att[...], wout_ref[...])).astype(bf16)
    pred = dot(bout[...], whead_ref[...]).astype(bf16).astype(f32).reshape(members, cells, chans)
    parts = []
    for c in range(CELLS):
        high = x_ref[c * 2, 0, :, half * width :].astype(f32)
        low = x_ref[c * 2 + 1, 0, :, half * width :].astype(f32)
        parts.append(high + low)
    target = jnp.concatenate(parts, axis=0)
    pair = [jnp.zeros((cells, chans), f32) for _ in range(members)]
    for a in range(members):
        for b in range(a + 1, members):
            s = slope(pred[a] - pred[b])
            pair[a] = pair[a] + s
            pair[b] = pair[b] - s
    for a in range(members):
        g_pred[a * cells : (a + 1) * cells, :] = (
            loss_scale / members * (slope(pred[a] - target) - pair[a] / (members - 1))
        ).astype(bf16)
    g_block[...] = dot_t(g_pred[...], whead_ref[...]).astype(bf16)
    g_att[...] = dot_t(g_block[...], wout_ref[...]).astype(bf16)

    @pl.loop(0, members)
    def _(m):
        at = pl.ds(pl.multiple_of(m * cells, cells), cells)
        mask = mask_ref[...]
        for p in range(packs):
            q = qkv[at, p * pack : (p + 1) * pack]
            k = qkv[at, width + p * pack : width + (p + 1) * pack]
            v = qkv[at, 2 * width + p * pack : 2 * width + (p + 1) * pack]
            upstream = expand(g_att[at, p * pack : (p + 1) * pack], mask)
            prob = probs[m, p]
            g_prob = dot_t(v, upstream)
            inner = jnp.sum(prob * g_prob, axis=0, keepdims=True)
            g_score = (prob * (g_prob - inner) * scale).astype(bf16)
            g_q = diagonal(dot_rows(g_score, k), lane, dim)
            g_k = dot(g_score, expand(q, mask))
            g_v = dot(prob.astype(bf16), upstream)
            g_qkv[at, p * pack : (p + 1) * pack] = g_q.astype(bf16)
            g_qkv[at, width + p * pack : width + (p + 1) * pack] = g_k.astype(bf16)
            g_qkv[at, 2 * width + p * pack : 2 * width + (p + 1) * pack] = g_v.astype(bf16)

    normed_t[...] = normed[...].T

    @pl.loop(0, 3 * width // tile)
    def _(n):
        at = pl.ds(pl.multiple_of(n * tile, tile), tile)
        acc[:, at] += dot(normed_t[...], g_qkv[:, at])

    normed_t[...] = att[...].T

    @pl.loop(0, width // tile)
    def _(n):
        at = pl.ds(pl.multiple_of(n * tile, tile), tile)
        there = pl.ds(pl.multiple_of(3 * width + n * tile, tile), tile)
        acc[:, there] += dot(normed_t[...], g_block[:, at])

    acc[:, 4 * width :] += dot_rows(bout[...], g_pred[...])

    @pl.loop(0, width // tile)
    def _(n):
        at = pl.ds(pl.multiple_of(n * tile, tile), tile)
        g_att[:, at] = dot_t(g_qkv[...], wqkv_ref[at, :]).astype(bf16)

    for m in range(members):
        x = xf[m * cells : (m + 1) * cells, :]
        centered = x - jnp.mean(x, axis=-1, keepdims=True)
        var = jnp.mean(centered * centered, axis=-1, keepdims=True)
        rstd = lax.rsqrt(var + eps_norm)
        xhat = centered * rstd
        h = g_att[m * cells : (m + 1) * cells, :].astype(f32) * gain
        grad = rstd * (
            h
            - jnp.mean(h, axis=-1, keepdims=True)
            - xhat * jnp.mean(h * xhat, axis=-1, keepdims=True)
        )
        grad = grad + g_block[m * cells : (m + 1) * cells, :].astype(f32)
        s, mm = m // half, m % half
        for c in range(CELLS):
            gx_ref[c * 2 + s, 0, :, mm * width : (mm + 1) * width] = grad[
                c * CELLS : (c + 1) * CELLS, :
            ].astype(bf16)

    @pl.when(step == pl.num_programs(0) - 1)
    def _():
        acc_ref[...] = acc[...].astype(acc_ref.dtype)


def block_call(x, gain, w_qkv, w_out, w_head, prev, last):
    sources, count, lat, lanes = x.shape
    width, chans = w_head.shape
    members = 2 * ((lanes - chans) // width)
    rows = members * CELLS * CELLS
    total = 4 * width + chans
    whole = lambda shape: pl.BlockSpec(shape, lambda i: (0,) * len(shape))
    in_specs = [
        pl.BlockSpec((sources, 1, lat, lanes), lambda i: (0, i, 0, 0)),
        whole((1, width)),
        whole(w_qkv.shape),
        whole(w_out.shape),
        whole(w_head.shape),
    ]
    args = [x, gain, w_qkv, w_out, w_head]
    if prev is not None:
        in_specs.append(whole((width, total)))
        args.append(prev)
    cells = CELLS * CELLS
    pack = 4 * (width // HEADS)
    return pl.pallas_call(
        functools.partial(block_kernel, members, width, chans, prev is None),
        grid=(count,),
        in_specs=in_specs,
        out_specs=[
            pl.BlockSpec((sources, 1, lat, lanes - chans), lambda i: (0, i, 0, 0)),
            whole((width, total)),
        ],
        out_shape=[
            jax.ShapeDtypeStruct((sources, count, lat, lanes - chans), bf16),
            jax.ShapeDtypeStruct((width, total), bf16 if last else f32),
        ],
        scratch_shapes=[
            pltpu.VMEM((rows, width), f32),
            pltpu.VMEM((rows, width), bf16),
            pltpu.VMEM((rows, width), bf16),
            pltpu.VMEM((rows, 3 * width), bf16),
            pltpu.VMEM((rows, 3 * width), bf16),
            pltpu.VMEM((rows, width), bf16),
            pltpu.VMEM((members, width // pack, cells, 4 * cells), f32),
            pltpu.VMEM((rows, width), bf16),
            pltpu.VMEM((rows, chans), bf16),
            pltpu.VMEM((rows, width), bf16),
            pltpu.VMEM((rows, width), bf16),
            pltpu.VMEM((4 * cells, pack), bf16),
            pltpu.VMEM((width, total), f32),
        ],
        compiler_params=pltpu.CompilerParams(vmem_limit_bytes=48 * 1024 * 1024),
        cost_estimate=pl.CostEstimate(
            flops=count * 8_000_000_000, bytes_accessed=16_000_000, transcendentals=1_000_000
        ),
        name="grid_block",
    )(*args)


def body(inputs, layer_norm_gain, w_qkv, w_out, w_head, target):
    members, lat, cols, width = inputs.shape
    chans = target.shape[-1]
    axes = ("col", "ens")
    owners = lax.axis_size("col") * lax.axis_size("ens")
    each = cols // owners
    gain = layer_norm_gain.reshape(1, width)
    high = lax.reduce_precision(target, 8, 7)
    target_part = jnp.where(lax.axis_index("ens") == 0, high, target - high).astype(bf16)
    send_x = inputs.reshape(members, lat, each, owners, width).transpose(2, 3, 1, 0, 4)
    send_x = send_x.reshape(each, owners, lat, members * width)
    send_t = target_part.reshape(lat, each, owners, chans).transpose(1, 2, 0, 3)
    send = jnp.concatenate([send_x, send_t], axis=-1)

    per = each // CHUNKS
    arrived = []
    for j in range(CHUNKS):
        part = send[j * per : (j + 1) * per].transpose(1, 0, 2, 3)
        arrived.append(lax.all_to_all(part, axes, split_axis=0, concat_axis=0, tiled=True))
    acc = None
    grads = []
    for j in range(CHUNKS):
        g, acc = block_call(arrived[j], gain, w_qkv, w_out, w_head, acc, j == CHUNKS - 1)
        grads.append(lax.all_to_all(g, axes, split_axis=0, concat_axis=0, tiled=True))
    grad = jnp.concatenate([g.transpose(1, 0, 2, 3) for g in grads], axis=0)
    grad_input = (
        grad.reshape(each, owners, lat, members, width)
        .transpose(3, 2, 0, 1, 4)
        .reshape(members, lat, cols, width)
    )
    share = lax.psum_scatter(acc, ("col", "spread"), scatter_dimension=0, tiled=True)
    share = lax.psum(share, "ens").astype(f32)
    grad_qkv = share[:, : 3 * width]
    grad_out = share[:, 3 * width : 4 * width]
    grad_head = share[:, 4 * width :]
    return (grad_input, grad_qkv, grad_out, grad_head)


def solution(mesh):
    groups, lon, ens = mesh.devices.shape
    split = Mesh(
        mesh.devices.reshape(groups, CELLS, lon // CELLS, ens), ("groups", "col", "spread", "ens")
    )
    lon_axes = ("col", "spread")
    in_specs = (
        P("ens", "groups", lon_axes, None),
        P(),
        P(),
        P(),
        P(),
        P("groups", lon_axes, None),
    )
    rows = P(("groups",) + lon_axes, None)
    out_specs = (P("ens", "groups", lon_axes, None), rows, rows, rows)
    return jax.shard_map(body, mesh=split, in_specs=in_specs, out_specs=out_specs, check_vma=False)
```

```python
import functools

import jax
import jax.numpy as jnp
from jax import lax
from jax.experimental import pallas as pl
from jax.experimental.pallas import tpu as pltpu
from jax.sharding import Mesh
from jax.sharding import PartitionSpec as P

HEADS = 16
CELLS = 8
eps_norm = 1e-05
smooth_width = 0.25
loss_scale = 32.0
LOG2E = 1.4426950408889634
CHUNKS = 2

bf16 = jnp.bfloat16
f32 = jnp.float32


def dot(left, right):
    return jnp.dot(left, right, preferred_element_type=f32)


def dot_t(left, right):
    return lax.dot_general(left, right, (((1,), (1,)), ((), ())), preferred_element_type=f32)


def dot_rows(left, right):
    return lax.dot_general(left, right, (((0,), (0,)), ((), ())), preferred_element_type=f32)


def slope(delta):
    return delta * lax.rsqrt(delta * delta + smooth_width * smooth_width)


def expand(block, mask):
    return jnp.concatenate([block] * 4, axis=0) * mask


def diagonal(wide, lane, dim):
    cells = wide.shape[0] // 4
    out = wide[:cells]
    for h in range(1, 4):
        out = jnp.where(lane >= h * dim, wide[h * cells : (h + 1) * cells], out)
    return out


def block_kernel(members, width, chans, first, *refs):
    if first:
        x_ref, gain_ref, wqkv_ref, wout_ref, whead_ref, gx_ref, acc_ref = refs[:7]
        scratch = refs[7:]
        prev_ref = None
    else:
        x_ref, gain_ref, wqkv_ref, wout_ref, whead_ref, prev_ref, gx_ref, acc_ref = refs[:8]
        scratch = refs[8:]
    xf, normed, normed_t, qkv, g_qkv, att, probs, bout, g_pred, g_block, g_att, mask_ref, acc = scratch
    cells = CELLS * CELLS
    rows = members * cells
    half = members // 2
    dim = width // HEADS
    pack = 4 * dim
    packs = width // pack
    scale = dim ** (-0.5)
    step = pl.program_id(0)
    tile = 256

    @pl.when(step == 0)
    def _():
        if first:
            acc[...] = jnp.zeros_like(acc)
        else:
            acc[...] = prev_ref[...]
        row_head = lax.broadcasted_iota(jnp.int32, (4 * cells, pack), 0) // cells
        lane_head = lax.broadcasted_iota(jnp.int32, (4 * cells, pack), 1) // dim
        mask_ref[...] = jnp.where(row_head == lane_head, 1.0, 0.0).astype(bf16)

    lane = lax.broadcasted_iota(jnp.int32, (cells, pack), 1)

    for c in range(CELLS):
        for s in range(2):
            for m in range(half):
                top = (s * half + m) * cells + c * CELLS
                xf[top : top + CELLS, :] = x_ref[
                    c * 2 + s, 0, :, m * width : (m + 1) * width
                ].astype(f32)

    gain = gain_ref[...]

    @pl.loop(0, members)
    def _(m):
        at = pl.ds(pl.multiple_of(m * cells, cells), cells)
        x = xf[at, :]
        centered = x - jnp.mean(x, axis=-1, keepdims=True)
        var = jnp.mean(centered * centered, axis=-1, keepdims=True)
        normed[at, :] = (centered * lax.rsqrt(var + eps_norm) * gain).astype(bf16)

    @pl.loop(0, 3 * width // tile)
    def _(n):
        at = pl.ds(pl.multiple_of(n * tile, tile), tile)
        qkv[:, at] = dot(normed[...], wqkv_ref[:, at]).astype(bf16)

    @pl.loop(0, members, unroll=8)
    def _(m):
        at = pl.ds(pl.multiple_of(m * cells, cells), cells)
        mask = mask_ref[...]
        each = range(packs)
        part = lambda p, i: qkv[at, i * width + p * pack : i * width + (p + 1) * pack]
        scores = [dot_t(part(p, 1), expand(part(p, 0), mask)) for p in each]
        expos = [
            jnp.exp2((s - jnp.max(s, axis=0, keepdims=True)) * (scale * LOG2E)) for s in scores
        ]
        weights = [e * (1.0 / jnp.sum(e, axis=0, keepdims=True)) for e in expos]
        for p in each:
            probs[m, p] = weights[p]
        outs = [dot_rows(weights[p].astype(bf16), part(p, 2)) for p in each]
        for p in each:
            att[at, p * pack : (p + 1) * pack] = diagonal(outs[p], lane, dim).astype(bf16)

    bout[...] = (xf[...] + dot(att[...], wout_ref[...])).astype(bf16)
    pred = dot(bout[...], whead_ref[...]).astype(bf16).astype(f32).reshape(members, cells, chans)
    parts = []
    for c in range(CELLS):
        high = x_ref[c * 2, 0, :, half * width :].astype(f32)
        low = x_ref[c * 2 + 1, 0, :, half * width :].astype(f32)
        parts.append(high + low)
    target = jnp.concatenate(parts, axis=0)
    pair = [jnp.zeros((cells, chans), f32) for _ in range(members)]
    for a in range(members):
        for b in range(a + 1, members):
            s = slope(pred[a] - pred[b])
            pair[a] = pair[a] + s
            pair[b] = pair[b] - s
    for a in range(members):
        g_pred[a * cells : (a + 1) * cells, :] = (
            loss_scale / members * (slope(pred[a] - target) - pair[a] / (members - 1))
        ).astype(bf16)
    g_block[...] = dot_t(g_pred[...], whead_ref[...]).astype(bf16)
    g_att[...] = dot_t(g_block[...], wout_ref[...]).astype(bf16)

    @pl.loop(0, members, unroll=8)
    def _(m):
        at = pl.ds(pl.multiple_of(m * cells, cells), cells)
        mask = mask_ref[...]
        each = range(packs)
        part = lambda p, i: qkv[at, i * width + p * pack : i * width + (p + 1) * pack]
        ups = [expand(g_att[at, p * pack : (p + 1) * pack], mask) for p in each]
        g_probs = [dot_t(part(p, 2), ups[p]) for p in each]
        g_vs = [dot(probs[m, p].astype(bf16), ups[p]) for p in each]
        g_scores = []
        for p in each:
            prob = probs[m, p]
            inner = jnp.sum(prob * g_probs[p], axis=0, keepdims=True)
            g_scores.append((prob * (g_probs[p] - inner) * scale).astype(bf16))
        g_qs = [dot_rows(g_scores[p], part(p, 1)) for p in each]
        g_ks = [dot(g_scores[p], expand(part(p, 0), mask)) for p in each]
        for p in each:
            at_p = lambda i: pl.ds(i * width + p * pack, pack)
            g_qkv[at, at_p(0)] = diagonal(g_qs[p], lane, dim).astype(bf16)
            g_qkv[at, at_p(1)] = g_ks[p].astype(bf16)
            g_qkv[at, at_p(2)] = g_vs[p].astype(bf16)

    normed_t[...] = normed[...].T

    @pl.loop(0, 3 * width // tile)
    def _(n):
        at = pl.ds(pl.multiple_of(n * tile, tile), tile)
        acc[:, at] += dot(normed_t[...], g_qkv[:, at])

    normed_t[...] = att[...].T

    @pl.loop(0, width // tile)
    def _(n):
        at = pl.ds(pl.multiple_of(n * tile, tile), tile)
        there = pl.ds(pl.multiple_of(3 * width + n * tile, tile), tile)
        acc[:, there] += dot(normed_t[...], g_block[:, at])

    acc[:, 4 * width :] += dot_rows(bout[...], g_pred[...])

    @pl.loop(0, width // tile)
    def _(n):
        at = pl.ds(pl.multiple_of(n * tile, tile), tile)
        g_att[:, at] = dot_t(g_qkv[...], wqkv_ref[at, :]).astype(bf16)

    for m in range(members):
        x = xf[m * cells : (m + 1) * cells, :]
        centered = x - jnp.mean(x, axis=-1, keepdims=True)
        var = jnp.mean(centered * centered, axis=-1, keepdims=True)
        rstd = lax.rsqrt(var + eps_norm)
        xhat = centered * rstd
        h = g_att[m * cells : (m + 1) * cells, :].astype(f32) * gain
        grad = rstd * (
            h
            - jnp.mean(h, axis=-1, keepdims=True)
            - xhat * jnp.mean(h * xhat, axis=-1, keepdims=True)
        )
        grad = grad + g_block[m * cells : (m + 1) * cells, :].astype(f32)
        s, mm = m // half, m % half
        for c in range(CELLS):
            gx_ref[c * 2 + s, 0, :, mm * width : (mm + 1) * width] = grad[
                c * CELLS : (c + 1) * CELLS, :
            ].astype(bf16)

    @pl.when(step == pl.num_programs(0) - 1)
    def _():
        acc_ref[...] = acc[...].astype(acc_ref.dtype)


def block_call(x, gain, w_qkv, w_out, w_head, prev, last):
    sources, count, lat, lanes = x.shape
    width, chans = w_head.shape
    members = 2 * ((lanes - chans) // width)
    rows = members * CELLS * CELLS
    total = 4 * width + chans
    whole = lambda shape: pl.BlockSpec(shape, lambda i: (0,) * len(shape))
    in_specs = [
        pl.BlockSpec((sources, 1, lat, lanes), lambda i: (0, i, 0, 0)),
        whole((1, width)),
        whole(w_qkv.shape),
        whole(w_out.shape),
        whole(w_head.shape),
    ]
    args = [x, gain, w_qkv, w_out, w_head]
    if prev is not None:
        in_specs.append(whole((width, total)))
        args.append(prev)
    cells = CELLS * CELLS
    pack = 4 * (width // HEADS)
    return pl.pallas_call(
        functools.partial(block_kernel, members, width, chans, prev is None),
        grid=(count,),
        in_specs=in_specs,
        out_specs=[
            pl.BlockSpec((sources, 1, lat, lanes - chans), lambda i: (0, i, 0, 0)),
            whole((width, total)),
        ],
        out_shape=[
            jax.ShapeDtypeStruct((sources, count, lat, lanes - chans), bf16),
            jax.ShapeDtypeStruct((width, total), bf16 if last else f32),
        ],
        scratch_shapes=[
            pltpu.VMEM((rows, width), f32),
            pltpu.VMEM((rows, width), bf16),
            pltpu.VMEM((rows, width), bf16),
            pltpu.VMEM((rows, 3 * width), bf16),
            pltpu.VMEM((rows, 3 * width), bf16),
            pltpu.VMEM((rows, width), bf16),
            pltpu.VMEM((members, width // pack, cells, 4 * cells), f32),
            pltpu.VMEM((rows, width), bf16),
            pltpu.VMEM((rows, chans), bf16),
            pltpu.VMEM((rows, width), bf16),
            pltpu.VMEM((rows, width), bf16),
            pltpu.VMEM((4 * cells, pack), bf16),
            pltpu.VMEM((width, total), f32),
        ],
        compiler_params=pltpu.CompilerParams(vmem_limit_bytes=48 * 1024 * 1024),
        cost_estimate=pl.CostEstimate(
            flops=count * 8_000_000_000, bytes_accessed=16_000_000, transcendentals=1_000_000
        ),
        name="grid_block",
    )(*args)


def swap_halves(pair, axes, bit, keep_first):
    count = 1
    for axis in axes:
        count *= lax.axis_size(axis)
    swap = [(i, i ^ bit) for i in range(count)]
    sent = lax.ppermute(jnp.where(keep_first, pair[1], pair[0]), axes, swap)
    kept = jnp.where(keep_first, pair[0], pair[1])
    return (kept.astype(f32) + sent.astype(f32)).astype(pair.dtype)


def reduce_rows(grad):
    lon = ("col", "spread")
    shards = lax.axis_size("col") * lax.axis_size("spread")
    me = lax.axis_index(lon)
    first = lax.axis_index("ens") == 0
    block = grad.shape[0] // shards
    rest = grad.reshape(shards, 2, block // 2, -1).transpose(1, 0, 2, 3)
    rest = swap_halves(rest, ("ens",), 1, first)
    bit = 1
    while bit < shards:
        left = rest.shape[0]
        pair = rest.reshape(left // 2, 2, *rest.shape[1:]).swapaxes(0, 1)
        rest = swap_halves(pair, lon, bit, (me // bit) % 2 == 0)
        bit *= 2
    share = rest[0]
    other = lax.ppermute(share, "ens", [(0, 1), (1, 0)])
    return jnp.concatenate(
        [jnp.where(first, share, other), jnp.where(first, other, share)], axis=0
    )


def body(inputs, layer_norm_gain, w_qkv, w_out, w_head, target):
    members, lat, cols, width = inputs.shape
    chans = target.shape[-1]
    axes = ("col", "ens")
    owners = lax.axis_size("col") * lax.axis_size("ens")
    each = cols // owners
    gain = layer_norm_gain.reshape(1, width)
    high = lax.reduce_precision(target, 8, 7)
    target_part = jnp.where(lax.axis_index("ens") == 0, high, target - high).astype(bf16)
    send_x = inputs.reshape(members, lat, each, owners, width).transpose(2, 3, 1, 0, 4)
    send_x = send_x.reshape(each, owners, lat, members * width)
    send_t = target_part.reshape(lat, each, owners, chans).transpose(1, 2, 0, 3)
    send = jnp.concatenate([send_x, send_t], axis=-1)

    per = each // CHUNKS
    arrived = []
    for j in range(CHUNKS):
        part = send[j * per : (j + 1) * per].transpose(1, 0, 2, 3)
        arrived.append(lax.all_to_all(part, axes, split_axis=0, concat_axis=0, tiled=True))
    acc = None
    grads = []
    for j in range(CHUNKS):
        g, acc = block_call(arrived[j], gain, w_qkv, w_out, w_head, acc, j == CHUNKS - 1)
        grads.append(lax.all_to_all(g, axes, split_axis=0, concat_axis=0, tiled=True))
    acc, *grads[:-1] = lax.optimization_barrier((acc, *grads[:-1]))
    grad = jnp.concatenate([g.transpose(1, 0, 2, 3) for g in grads], axis=0)
    grad_input = (
        grad.reshape(each, owners, lat, members, width)
        .transpose(3, 2, 0, 1, 4)
        .reshape(members, lat, cols, width)
    )
    share = reduce_rows(acc).astype(f32)
    grad_qkv = share[:, : 3 * width]
    grad_out = share[:, 3 * width : 4 * width]
    grad_head = share[:, 4 * width :]
    return (grad_input, grad_qkv, grad_out, grad_head)


def solution(mesh):
    groups, lon, ens = mesh.devices.shape
    split = Mesh(
        mesh.devices.reshape(groups, CELLS, lon // CELLS, ens), ("groups", "col", "spread", "ens")
    )
    lon_axes = ("col", "spread")
    in_specs = (
        P("ens", "groups", lon_axes, None),
        P(),
        P(),
        P(),
        P(),
        P("groups", lon_axes, None),
    )
    rows = P(("groups",) + lon_axes, None)
    out_specs = (P("ens", "groups", lon_axes, None), rows, rows, rows)
    return jax.shard_map(body, mesh=split, in_specs=in_specs, out_specs=out_specs, check_vma=False)
```

```python
import functools

import jax
import jax.numpy as jnp
from jax import lax
from jax.experimental import pallas as pl
from jax.experimental.pallas import tpu as pltpu
from jax.sharding import Mesh
from jax.sharding import PartitionSpec as P

HEADS = 16
CELLS = 8
eps_norm = 1e-05
smooth_width = 0.25
loss_scale = 32.0
LOG2E = 1.4426950408889634
TIE_EARLY = 1
TIE_LATE = 4

bf16 = jnp.bfloat16
f32 = jnp.float32


def dot(left, right):
    return jnp.dot(left, right, preferred_element_type=f32)


def dot_t(left, right):
    return lax.dot_general(left, right, (((1,), (1,)), ((), ())), preferred_element_type=f32)


def dot_rows(left, right):
    return lax.dot_general(left, right, (((0,), (0,)), ((), ())), preferred_element_type=f32)


def slope(delta):
    return delta * lax.rsqrt(delta * delta + smooth_width * smooth_width)


def expand(block, mask):
    return jnp.concatenate([block] * 4, axis=0) * mask


def diagonal(wide, lane, dim):
    cells = wide.shape[0] // 4
    out = wide[:cells]
    for h in range(1, 4):
        out = jnp.where(lane >= h * dim, wide[h * cells : (h + 1) * cells], out)
    return out


def block_kernel(members, width, chans, first, last, *refs):
    x_ref, gain_ref, wqkv_hbm, wout_hbm, whead_hbm = refs[:5]
    refs = refs[5:]
    if not first:
        prev_ref, refs = refs[0], refs[1:]
    gx_ref, refs = refs[0], refs[1:]
    if last:
        mine_ref, sent_ref, refs = refs[0], refs[1], refs[2:]
    else:
        acc_ref, refs = refs[0], refs[1:]
    xf, normed, normed_t, qkv, g_qkv, att, probs, bout, g_pred, g_block, g_att, mask_ref, acc = (
        refs[:13]
    )
    wqkv_ref, wout_ref, whead_ref, sems = refs[13:]
    fetches = [
        pltpu.make_async_copy(wqkv_hbm, wqkv_ref, sems.at[0]),
        pltpu.make_async_copy(wout_hbm, wout_ref, sems.at[1]),
        pltpu.make_async_copy(whead_hbm, whead_ref, sems.at[2]),
    ]
    if not first:
        fetches.append(pltpu.make_async_copy(prev_ref, acc, sems.at[3]))
    cells = CELLS * CELLS
    rows = members * cells
    half = members // 2
    dim = width // HEADS
    pack = 4 * dim
    packs = width // pack
    scale = dim ** (-0.5)
    step = pl.program_id(0)
    tile = 256

    @pl.when(step == 0)
    def _():
        for fetch in fetches:
            fetch.start()
        if first:
            acc[...] = jnp.zeros_like(acc)
        row_head = lax.broadcasted_iota(jnp.int32, (4 * cells, pack), 0) // cells
        lane_head = lax.broadcasted_iota(jnp.int32, (4 * cells, pack), 1) // dim
        mask_ref[...] = jnp.where(row_head == lane_head, 1.0, 0.0).astype(bf16)

    lane = lax.broadcasted_iota(jnp.int32, (cells, pack), 1)

    for c in range(CELLS):
        for s in range(2):
            for m in range(half):
                top = (s * half + m) * cells + c * CELLS
                xf[top : top + CELLS, :] = x_ref[
                    c * 2 + s, 0, :, m * width : (m + 1) * width
                ].astype(f32)

    gain = gain_ref[...]

    @pl.loop(0, members)
    def _(m):
        at = pl.ds(pl.multiple_of(m * cells, cells), cells)
        x = xf[at, :]
        centered = x - jnp.mean(x, axis=-1, keepdims=True)
        var = jnp.mean(centered * centered, axis=-1, keepdims=True)
        normed[at, :] = (centered * lax.rsqrt(var + eps_norm) * gain).astype(bf16)

    @pl.when(step == 0)
    def _():
        fetches[0].wait()

    @pl.loop(0, 3 * width // tile)
    def _(n):
        at = pl.ds(pl.multiple_of(n * tile, tile), tile)
        qkv[:, at] = dot(normed[...], wqkv_ref[:, at]).astype(bf16)

    @pl.loop(0, members, unroll=8)
    def _(m):
        at = pl.ds(pl.multiple_of(m * cells, cells), cells)
        mask = mask_ref[...]
        each = range(packs)
        part = lambda p, i: qkv[at, i * width + p * pack : i * width + (p + 1) * pack]
        scores = [dot_t(part(p, 1), expand(part(p, 0), mask)) for p in each]
        expos = [
            jnp.exp2((s - jnp.max(s, axis=0, keepdims=True)) * (scale * LOG2E)) for s in scores
        ]
        weights = [e * (1.0 / jnp.sum(e, axis=0, keepdims=True)) for e in expos]
        for p in each:
            probs[m, p] = weights[p]
        outs = [dot_rows(weights[p].astype(bf16), part(p, 2)) for p in each]
        for p in each:
            att[at, p * pack : (p + 1) * pack] = diagonal(outs[p], lane, dim).astype(bf16)

    @pl.when(step == 0)
    def _():
        for fetch in fetches[1:]:
            fetch.wait()

    bout[...] = (xf[...] + dot(att[...], wout_ref[...])).astype(bf16)
    pred = dot(bout[...], whead_ref[...]).astype(bf16).astype(f32).reshape(members, cells, chans)
    parts = []
    for c in range(CELLS):
        high = x_ref[c * 2, 0, :, half * width :].astype(f32)
        low = x_ref[c * 2 + 1, 0, :, half * width :].astype(f32)
        parts.append(high + low)
    target = jnp.concatenate(parts, axis=0)
    pair = [jnp.zeros((cells, chans), f32) for _ in range(members)]
    for a in range(members):
        for b in range(a + 1, members):
            s = slope(pred[a] - pred[b])
            pair[a] = pair[a] + s
            pair[b] = pair[b] - s
    for a in range(members):
        g_pred[a * cells : (a + 1) * cells, :] = (
            loss_scale / members * (slope(pred[a] - target) - pair[a] / (members - 1))
        ).astype(bf16)
    g_block[...] = dot_t(g_pred[...], whead_ref[...]).astype(bf16)
    g_att[...] = dot_t(g_block[...], wout_ref[...]).astype(bf16)

    @pl.loop(0, members, unroll=8)
    def _(m):
        at = pl.ds(pl.multiple_of(m * cells, cells), cells)
        mask = mask_ref[...]
        each = range(packs)
        part = lambda p, i: qkv[at, i * width + p * pack : i * width + (p + 1) * pack]
        ups = [expand(g_att[at, p * pack : (p + 1) * pack], mask) for p in each]
        g_probs = [dot_t(part(p, 2), ups[p]) for p in each]
        g_vs = [dot(probs[m, p].astype(bf16), ups[p]) for p in each]
        g_scores = []
        for p in each:
            prob = probs[m, p]
            inner = jnp.sum(prob * g_probs[p], axis=0, keepdims=True)
            g_scores.append((prob * (g_probs[p] - inner) * scale).astype(bf16))
        g_qs = [dot_rows(g_scores[p], part(p, 1)) for p in each]
        g_ks = [dot(g_scores[p], expand(part(p, 0), mask)) for p in each]
        for p in each:
            at_p = lambda i: pl.ds(i * width + p * pack, pack)
            g_qkv[at, at_p(0)] = diagonal(g_qs[p], lane, dim).astype(bf16)
            g_qkv[at, at_p(1)] = g_ks[p].astype(bf16)
            g_qkv[at, at_p(2)] = g_vs[p].astype(bf16)

    normed_t[...] = normed[...].T

    @pl.loop(0, 3 * width // tile)
    def _(n):
        at = pl.ds(pl.multiple_of(n * tile, tile), tile)
        acc[:, at] += dot(normed_t[...], g_qkv[:, at])

    normed_t[...] = att[...].T

    @pl.loop(0, width // tile)
    def _(n):
        at = pl.ds(pl.multiple_of(n * tile, tile), tile)
        there = pl.ds(pl.multiple_of(3 * width + n * tile, tile), tile)
        acc[:, there] += dot(normed_t[...], g_block[:, at])

    acc[:, 4 * width :] += dot_rows(bout[...], g_pred[...])

    @pl.when(step == pl.num_programs(0) - 1)
    def _():
        if last:
            core = lax.axis_index("ens")
            shards, piece, _ = mine_ref.shape
            for b in range(shards):
                low = acc[2 * b * piece : (2 * b + 1) * piece, :]
                high = acc[(2 * b + 1) * piece : (2 * b + 2) * piece, :]
                mine_ref[b] = jnp.where(core == 0, low, high).astype(bf16)
                sent_ref[b] = jnp.where(core == 0, high, low).astype(bf16)
        else:
            pltpu.make_async_copy(acc, acc_ref, sems.at[3]).start()

    @pl.loop(0, width // tile)
    def _(n):
        at = pl.ds(pl.multiple_of(n * tile, tile), tile)
        g_att[:, at] = dot_t(g_qkv[...], wqkv_ref[at, :]).astype(bf16)

    for m in range(members):
        x = xf[m * cells : (m + 1) * cells, :]
        centered = x - jnp.mean(x, axis=-1, keepdims=True)
        var = jnp.mean(centered * centered, axis=-1, keepdims=True)
        rstd = lax.rsqrt(var + eps_norm)
        xhat = centered * rstd
        h = g_att[m * cells : (m + 1) * cells, :].astype(f32) * gain
        grad = rstd * (
            h
            - jnp.mean(h, axis=-1, keepdims=True)
            - xhat * jnp.mean(h * xhat, axis=-1, keepdims=True)
        )
        grad = grad + g_block[m * cells : (m + 1) * cells, :].astype(f32)
        s, mm = m // half, m % half
        for c in range(CELLS):
            gx_ref[c * 2 + s, 0, :, mm * width : (mm + 1) * width] = grad[
                c * CELLS : (c + 1) * CELLS, :
            ].astype(bf16)

    if not last:

        @pl.when(step == pl.num_programs(0) - 1)
        def _():
            pltpu.make_async_copy(acc, acc_ref, sems.at[3]).wait()


def block_call(x, gain, w_qkv, w_out, w_head, prev, shards):
    sources, count, lat = x.shape[:3]
    width, chans = w_head.shape
    members = 8
    lanes = members // 2 * width
    rows = members * CELLS * CELLS
    total = 4 * width + chans
    whole = lambda shape: pl.BlockSpec(shape, lambda i: (0,) * len(shape))
    anywhere = pl.BlockSpec(memory_space=pl.ANY)
    in_specs = [
        pl.BlockSpec((sources, 1, lat, lanes + chans), lambda i: (0, i, 0, 0)),
        whole((1, width)),
        anywhere,
        anywhere,
        anywhere,
    ]
    args = [x, gain, w_qkv, w_out, w_head]
    if prev is not None:
        in_specs.append(anywhere)
        args.append(prev)
    cells = CELLS * CELLS
    pack = 4 * (width // HEADS)
    out_specs = [pl.BlockSpec((sources, 1, lat, lanes), lambda i: (0, i, 0, 0))]
    out_shape = [jax.ShapeDtypeStruct((sources, count, lat, lanes), bf16)]
    if shards:
        sums = (shards, width // shards // 2, total)
        out_specs += [whole(sums)] * 2
        out_shape += [jax.ShapeDtypeStruct(sums, bf16)] * 2
    else:
        out_specs.append(anywhere)
        out_shape.append(jax.ShapeDtypeStruct((width, total), f32))
    return pl.pallas_call(
        functools.partial(block_kernel, members, width, chans, prev is None, shards > 0),
        grid=(count,),
        in_specs=in_specs,
        out_specs=out_specs,
        out_shape=out_shape,
        scratch_shapes=[
            pltpu.VMEM((rows, width), f32),
            pltpu.VMEM((rows, width), bf16),
            pltpu.VMEM((rows, width), bf16),
            pltpu.VMEM((rows, 3 * width), bf16),
            pltpu.VMEM((rows, 3 * width), bf16),
            pltpu.VMEM((rows, width), bf16),
            pltpu.VMEM((members, width // pack, cells, 4 * cells), f32),
            pltpu.VMEM((rows, width), bf16),
            pltpu.VMEM((rows, chans), bf16),
            pltpu.VMEM((rows, width), bf16),
            pltpu.VMEM((rows, width), bf16),
            pltpu.VMEM((4 * cells, pack), bf16),
            pltpu.VMEM((width, total), f32),
            pltpu.VMEM(w_qkv.shape, bf16),
            pltpu.VMEM(w_out.shape, bf16),
            pltpu.VMEM(w_head.shape, bf16),
            pltpu.SemaphoreType.DMA((4,)),
        ],
        compiler_params=pltpu.CompilerParams(vmem_limit_bytes=48 * 1024 * 1024),
        cost_estimate=pl.CostEstimate(
            flops=count * 8_000_000_000, bytes_accessed=16_000_000, transcendentals=1_000_000
        ),
        name="grid_block",
    )(*args)


def swap_halves(pair, axes, bit, keep_first):
    kept = jnp.where(keep_first, pair[0], pair[1])
    return swap_sum(kept, jnp.where(keep_first, pair[1], pair[0]), axes, bit)


def swap_sum(kept, given, axes, bit):
    count = 1
    for axis in axes:
        count *= lax.axis_size(axis)
    swap = [(i, i ^ bit) for i in range(count)]
    taken = lax.ppermute(given, axes, swap)
    return (kept.astype(f32) + taken.astype(f32)).astype(kept.dtype)


def reduce_rows(mine, given, early, late):
    lon = ("col", "spread")
    shards = lax.axis_size("col") * lax.axis_size("spread")
    me = lax.axis_index(lon)
    first = lax.axis_index("ens") == 0
    rest = swap_sum(mine, given, ("ens",), 1)
    bit = 1
    while bit < shards:
        left = rest.shape[0]
        pair = rest.reshape(left // 2, 2, *rest.shape[1:]).swapaxes(0, 1)
        if bit == TIE_EARLY:
            pair, early = lax.optimization_barrier((pair, early))
        if bit == TIE_LATE:
            pair, late = lax.optimization_barrier((pair, late))
        rest = swap_halves(pair, lon, bit, (me // bit) % 2 == 0)
        bit *= 2
    share = rest[0]
    if TIE_LATE is None:
        share, late = lax.optimization_barrier((share, late))
    other = lax.ppermute(share, "ens", [(0, 1), (1, 0)])
    share = jnp.concatenate(
        [jnp.where(first, share, other), jnp.where(first, other, share)], axis=0
    )
    return share, early, late


def body(inputs, layer_norm_gain, w_qkv, w_out, w_head, target):
    members, lat, cols, width = inputs.shape
    chans = target.shape[-1]
    axes = ("col", "ens")
    owners = lax.axis_size("col") * lax.axis_size("ens")
    each = cols // owners
    shards = lax.axis_size("col") * lax.axis_size("spread")
    gain = layer_norm_gain.reshape(1, width)
    lanes = members * width
    move = lambda g: lax.all_to_all(g, axes, split_axis=0, concat_axis=0, tiled=True)
    high = lax.reduce_precision(target, 8, 7)
    target_part = jnp.where(lax.axis_index("ens") == 0, high, target - high).astype(bf16)

    def outgoing(start, count):
        span = slice(start * owners, (start + count) * owners)
        send_x = inputs[:, :, span].reshape(members, lat, count, owners, width)
        send_x = send_x.transpose(3, 2, 1, 0, 4).reshape(owners, count, lat, lanes)
        send_t = target_part[:, span].reshape(lat, count, owners, chans).transpose(2, 1, 0, 3)
        return jnp.concatenate([send_x, send_t], axis=-1)

    lead, main = each // 4, each // 2
    tail = each - lead - main
    x_lead = move(outgoing(0, lead))
    x_main = move(outgoing(lead, main))
    weights = (gain, w_qkv, w_out, w_head)
    g_lead, acc = block_call(x_lead, *weights, None, 0)
    both = move(jnp.concatenate([outgoing(lead + main, tail), g_lead], axis=-1))
    g_main, acc = block_call(x_main, *weights, acc, 0)
    g_main = move(g_main)
    g_tail, mine, given = block_call(both, *weights, acc, shards)
    g_tail = move(g_tail)
    back_lead = both[..., lanes + chans :]
    share, (g_main,), g_tail = reduce_rows(mine, given, [g_main], g_tail)
    share = share.astype(f32)
    columns = (
        lambda g: g.reshape(owners, -1, lat, members, width)
        .transpose(3, 2, 1, 0, 4)
        .reshape(members, lat, -1, width)
    )
    ready = jnp.concatenate([columns(back_lead), columns(g_main)], axis=2)
    ready = jnp.pad(ready, ((0, 0), (0, 0), (0, tail * owners), (0, 0)))
    ready = lax.optimization_barrier(ready)
    grad_input = lax.dynamic_update_slice(
        ready, columns(g_tail), (0, 0, (lead + main) * owners, 0)
    )
    grad_qkv = share[:, : 3 * width]
    grad_out = share[:, 3 * width : 4 * width]
    grad_head = share[:, 4 * width :]
    return (grad_input, grad_qkv, grad_out, grad_head)


def solution(mesh):
    groups, lon, ens = mesh.devices.shape
    split = Mesh(
        mesh.devices.reshape(groups, CELLS, lon // CELLS, ens), ("groups", "col", "spread", "ens")
    )
    lon_axes = ("col", "spread")
    in_specs = (
        P("ens", "groups", lon_axes, None),
        P(),
        P(),
        P(),
        P(),
        P("groups", lon_axes, None),
    )
    rows = P(("groups",) + lon_axes, None)
    out_specs = (P("ens", "groups", lon_axes, None), rows, rows, rows)
    return jax.shard_map(body, mesh=split, in_specs=in_specs, out_specs=out_specs, check_vma=False)
```

```python
import functools

import jax
import jax.numpy as jnp
from jax import lax
from jax.experimental import pallas as pl
from jax.experimental.pallas import tpu as pltpu
from jax.sharding import Mesh
from jax.sharding import PartitionSpec as P

HEADS = 16
CELLS = 8
eps_norm = 1e-05
smooth_width = 0.25
loss_scale = 32.0
LOG2E = 1.4426950408889634
LATE = 3

bf16 = jnp.bfloat16
f32 = jnp.float32


def dot(left, right):
    return jnp.dot(left, right, preferred_element_type=f32)


def dot_t(left, right):
    return lax.dot_general(left, right, (((1,), (1,)), ((), ())), preferred_element_type=f32)


def dot_rows(left, right):
    return lax.dot_general(left, right, (((0,), (0,)), ((), ())), preferred_element_type=f32)


def slope(delta):
    return delta * lax.rsqrt(delta * delta + smooth_width * smooth_width)


def expand(block, mask):
    return jnp.concatenate([block] * 4, axis=0) * mask


def diagonal(wide, lane, dim):
    cells = wide.shape[0] // 4
    out = wide[:cells]
    for h in range(1, 4):
        out = jnp.where(lane >= h * dim, wide[h * cells : (h + 1) * cells], out)
    return out


def block_kernel(members, width, chans, first, last, *refs):
    x_ref, gain_ref, wqkv_hbm, wout_hbm, whead_hbm = refs[:5]
    refs = refs[5:]
    if not first:
        prev_ref, refs = refs[0], refs[1:]
    gx_ref, refs = refs[0], refs[1:]
    if last:
        sum_refs, refs = refs[:4], refs[4:]
    else:
        acc_ref, refs = refs[0], refs[1:]
    xf, normed, normed_t, qkv, g_qkv, att, probs, bout, g_pred, g_block, g_att, mask_ref, acc = (
        refs[:13]
    )
    wqkv_ref, wout_ref, whead_ref, sems = refs[13:]
    fetches = [
        pltpu.make_async_copy(wqkv_hbm, wqkv_ref, sems.at[0]),
        pltpu.make_async_copy(wout_hbm, wout_ref, sems.at[1]),
        pltpu.make_async_copy(whead_hbm, whead_ref, sems.at[2]),
    ]
    if not first:
        fetches.append(pltpu.make_async_copy(prev_ref, acc, sems.at[3]))
    cells = CELLS * CELLS
    rows = members * cells
    half = members // 2
    dim = width // HEADS
    pack = 4 * dim
    packs = width // pack
    scale = dim ** (-0.5)
    step = pl.program_id(0)
    tile = 256

    @pl.when(step == 0)
    def _():
        for fetch in fetches:
            fetch.start()
        if first:
            acc[...] = jnp.zeros_like(acc)
        row_head = lax.broadcasted_iota(jnp.int32, (4 * cells, pack), 0) // cells
        lane_head = lax.broadcasted_iota(jnp.int32, (4 * cells, pack), 1) // dim
        mask_ref[...] = jnp.where(row_head == lane_head, 1.0, 0.0).astype(bf16)

    lane = lax.broadcasted_iota(jnp.int32, (cells, pack), 1)

    for c in range(CELLS):
        for s in range(2):
            for m in range(half):
                top = (s * half + m) * cells + c * CELLS
                xf[top : top + CELLS, :] = x_ref[
                    c * 2 + s, 0, :, m * width : (m + 1) * width
                ].astype(f32)

    gain = gain_ref[...]

    @pl.loop(0, members, unroll=True)
    def _(m):
        at = pl.ds(pl.multiple_of(m * cells, cells), cells)
        x = xf[at, :]
        centered = x - jnp.mean(x, axis=-1, keepdims=True)
        var = jnp.mean(centered * centered, axis=-1, keepdims=True)
        normed[at, :] = (centered * lax.rsqrt(var + eps_norm) * gain).astype(bf16)

    @pl.when(step == 0)
    def _():
        fetches[0].wait()

    @pl.loop(0, 3 * width // tile, unroll=True)
    def _(n):
        at = pl.ds(pl.multiple_of(n * tile, tile), tile)
        qkv[:, at] = dot(normed[...], wqkv_ref[:, at]).astype(bf16)

    @pl.loop(0, members, unroll=8)
    def _(m):
        at = pl.ds(pl.multiple_of(m * cells, cells), cells)
        mask = mask_ref[...]
        each = range(packs)
        part = lambda p, i: qkv[at, i * width + p * pack : i * width + (p + 1) * pack]
        scores = [dot_t(part(p, 1), expand(part(p, 0), mask)) for p in each]
        expos = [
            jnp.exp2((s - jnp.max(s, axis=0, keepdims=True)) * (scale * LOG2E)) for s in scores
        ]
        weights = [e * (1.0 / jnp.sum(e, axis=0, keepdims=True)) for e in expos]
        for p in each:
            probs[m, p] = weights[p]
        outs = [dot_rows(weights[p].astype(bf16), part(p, 2)) for p in each]
        for p in each:
            att[at, p * pack : (p + 1) * pack] = diagonal(outs[p], lane, dim).astype(bf16)

    @pl.when(step == 0)
    def _():
        for fetch in fetches[1:]:
            fetch.wait()

    bout[...] = (xf[...] + dot(att[...], wout_ref[...])).astype(bf16)
    pred = dot(bout[...], whead_ref[...]).astype(bf16).astype(f32).reshape(members, cells, chans)
    parts = []
    for c in range(CELLS):
        high = x_ref[c * 2, 0, :, half * width :].astype(f32)
        low = x_ref[c * 2 + 1, 0, :, half * width :].astype(f32)
        parts.append(high + low)
    target = jnp.concatenate(parts, axis=0)
    pair = [jnp.zeros((cells, chans), f32) for _ in range(members)]
    for a in range(members):
        for b in range(a + 1, members):
            s = slope(pred[a] - pred[b])
            pair[a] = pair[a] + s
            pair[b] = pair[b] - s
    for a in range(members):
        g_pred[a * cells : (a + 1) * cells, :] = (
            loss_scale / members * (slope(pred[a] - target) - pair[a] / (members - 1))
        ).astype(bf16)
    g_block[...] = dot_t(g_pred[...], whead_ref[...]).astype(bf16)
    g_att[...] = dot_t(g_block[...], wout_ref[...]).astype(bf16)

    @pl.loop(0, members, unroll=8)
    def _(m):
        at = pl.ds(pl.multiple_of(m * cells, cells), cells)
        mask = mask_ref[...]
        each = range(packs)
        part = lambda p, i: qkv[at, i * width + p * pack : i * width + (p + 1) * pack]
        ups = [expand(g_att[at, p * pack : (p + 1) * pack], mask) for p in each]
        g_probs = [dot_t(part(p, 2), ups[p]) for p in each]
        g_vs = [dot(probs[m, p].astype(bf16), ups[p]) for p in each]
        g_scores = []
        for p in each:
            prob = probs[m, p]
            inner = jnp.sum(prob * g_probs[p], axis=0, keepdims=True)
            g_scores.append((prob * (g_probs[p] - inner) * scale).astype(bf16))
        g_qs = [dot_rows(g_scores[p], part(p, 1)) for p in each]
        g_ks = [dot(g_scores[p], expand(part(p, 0), mask)) for p in each]
        for p in each:
            at_p = lambda i: pl.ds(i * width + p * pack, pack)
            g_qkv[at, at_p(0)] = diagonal(g_qs[p], lane, dim).astype(bf16)
            g_qkv[at, at_p(1)] = g_ks[p].astype(bf16)
            g_qkv[at, at_p(2)] = g_vs[p].astype(bf16)

    normed_t[...] = normed[...].T

    @pl.loop(0, 3 * width // tile, unroll=True)
    def _(n):
        at = pl.ds(pl.multiple_of(n * tile, tile), tile)
        acc[:, at] += dot(normed_t[...], g_qkv[:, at])

    normed_t[...] = att[...].T

    @pl.loop(0, width // tile, unroll=True)
    def _(n):
        at = pl.ds(pl.multiple_of(n * tile, tile), tile)
        there = pl.ds(pl.multiple_of(3 * width + n * tile, tile), tile)
        acc[:, there] += dot(normed_t[...], g_block[:, at])

    acc[:, 4 * width :] += dot_rows(bout[...], g_pred[...])

    @pl.when(step == pl.num_programs(0) - 1)
    def _():
        if last:
            core = lax.axis_index("ens")
            shards, piece, cut = sum_refs[0].shape
            for b in range(shards):
                for i, span in enumerate((slice(0, cut), slice(cut, acc.shape[1]))):
                    low = acc[2 * b * piece : (2 * b + 1) * piece, span]
                    high = acc[(2 * b + 1) * piece : (2 * b + 2) * piece, span]
                    sum_refs[2 * i][b] = jnp.where(core == 0, low, high).astype(bf16)
                    sum_refs[2 * i + 1][b] = jnp.where(core == 0, high, low).astype(bf16)
        else:
            pltpu.make_async_copy(acc, acc_ref, sems.at[3]).start()

    @pl.loop(0, width // tile, unroll=True)
    def _(n):
        at = pl.ds(pl.multiple_of(n * tile, tile), tile)
        g_att[:, at] = dot_t(g_qkv[...], wqkv_ref[at, :]).astype(bf16)

    for m in range(members):
        x = xf[m * cells : (m + 1) * cells, :]
        centered = x - jnp.mean(x, axis=-1, keepdims=True)
        var = jnp.mean(centered * centered, axis=-1, keepdims=True)
        rstd = lax.rsqrt(var + eps_norm)
        xhat = centered * rstd
        h = g_att[m * cells : (m + 1) * cells, :].astype(f32) * gain
        grad = rstd * (
            h
            - jnp.mean(h, axis=-1, keepdims=True)
            - xhat * jnp.mean(h * xhat, axis=-1, keepdims=True)
        )
        grad = grad + g_block[m * cells : (m + 1) * cells, :].astype(f32)
        s, mm = m // half, m % half
        for c in range(CELLS):
            gx_ref[c * 2 + s, 0, :, mm * width : (mm + 1) * width] = grad[
                c * CELLS : (c + 1) * CELLS, :
            ].astype(bf16)

    if not last:

        @pl.when(step == pl.num_programs(0) - 1)
        def _():
            pltpu.make_async_copy(acc, acc_ref, sems.at[3]).wait()


def block_call(x, gain, w_qkv, w_out, w_head, prev, shards):
    sources, count, lat = x.shape[:3]
    width, chans = w_head.shape
    members = 8
    lanes = members // 2 * width
    rows = members * CELLS * CELLS
    total = 4 * width + chans
    whole = lambda shape: pl.BlockSpec(shape, lambda i: (0,) * len(shape))
    anywhere = pl.BlockSpec(memory_space=pl.ANY)
    in_specs = [
        pl.BlockSpec((sources, 1, lat, lanes + chans), lambda i: (0, i, 0, 0)),
        whole((1, width)),
        anywhere,
        anywhere,
        anywhere,
    ]
    args = [x, gain, w_qkv, w_out, w_head]
    if prev is not None:
        in_specs.append(anywhere)
        args.append(prev)
    cells = CELLS * CELLS
    pack = 4 * (width // HEADS)
    out_specs = [pl.BlockSpec((sources, 1, lat, lanes), lambda i: (0, i, 0, 0))]
    out_shape = [jax.ShapeDtypeStruct((sources, count, lat, lanes), bf16)]
    if shards:
        cut = total // 256 * 128
        for part in (cut, cut, total - cut, total - cut):
            sums = (shards, width // shards // 2, part)
            out_specs.append(whole(sums))
            out_shape.append(jax.ShapeDtypeStruct(sums, bf16))
    else:
        out_specs.append(anywhere)
        out_shape.append(jax.ShapeDtypeStruct((width, total), f32))
    return pl.pallas_call(
        functools.partial(block_kernel, members, width, chans, prev is None, shards > 0),
        grid=(count,),
        in_specs=in_specs,
        out_specs=out_specs,
        out_shape=out_shape,
        scratch_shapes=[
            pltpu.VMEM((rows, width), f32),
            pltpu.VMEM((rows, width), bf16),
            pltpu.VMEM((rows, width), bf16),
            pltpu.VMEM((rows, 3 * width), bf16),
            pltpu.VMEM((rows, 3 * width), bf16),
            pltpu.VMEM((rows, width), bf16),
            pltpu.VMEM((members, width // pack, cells, 4 * cells), f32),
            pltpu.VMEM((rows, width), bf16),
            pltpu.VMEM((rows, chans), bf16),
            pltpu.VMEM((rows, width), bf16),
            pltpu.VMEM((rows, width), bf16),
            pltpu.VMEM((4 * cells, pack), bf16),
            pltpu.VMEM((width, total), f32),
            pltpu.VMEM(w_qkv.shape, bf16),
            pltpu.VMEM(w_out.shape, bf16),
            pltpu.VMEM(w_head.shape, bf16),
            pltpu.SemaphoreType.DMA((4,)),
        ],
        compiler_params=pltpu.CompilerParams(vmem_limit_bytes=60 * 1024 * 1024),
        cost_estimate=pl.CostEstimate(
            flops=count * 8_000_000_000, bytes_accessed=16_000_000, transcendentals=1_000_000
        ),
        name="grid_block",
    )(*args)


def swap_sum(kept, given, axes, bit):
    count = 1
    for axis in axes:
        count *= lax.axis_size(axis)
    taken = lax.ppermute(given, axes, [(i, i ^ bit) for i in range(count)])
    return (kept.astype(f32) + taken.astype(f32)).astype(kept.dtype)


def reduce_rows(sums, early, late):
    lon = ("col", "spread")
    shards = lax.axis_size("col") * lax.axis_size("spread")
    bits = shards.bit_length() - 1
    assert shards == 1 << bits
    me = lax.axis_index(lon)
    first = lax.axis_index("ens") == 0
    (*sums, early) = lax.optimization_barrier((*sums, early))
    rest = [swap_sum(mine, given, ("ens",), 1) for mine, given in sums]
    rest = [r.reshape((2,) * bits + r.shape[1:]) for r in rest]
    orders = [list(range(bits)), [1, 0] + list(range(2, bits))]
    left = [list(range(bits))[::-1] for _ in orders]
    for i in range(bits):
        if i == LATE:
            *rest, late = lax.optimization_barrier((*rest, late))
        for c, order in enumerate(orders):
            axis = left[c].index(order[i])
            left[c].remove(order[i])
            low, high = (lax.index_in_dim(rest[c], h, axis, keepdims=False) for h in range(2))
            mine = (me >> order[i]) % 2 == 0
            rest[c] = swap_sum(
                jnp.where(mine, low, high), jnp.where(mine, high, low), lon, 1 << order[i]
            )
    if LATE >= bits:
        *rest, late = lax.optimization_barrier((*rest, late))
    share = jnp.concatenate(rest, axis=-1)
    other = lax.ppermute(share, "ens", [(0, 1), (1, 0)])
    share = jnp.concatenate(
        [jnp.where(first, share, other), jnp.where(first, other, share)], axis=0
    )
    return share, early, late


def body(inputs, layer_norm_gain, w_qkv, w_out, w_head, target):
    members, lat, cols, width = inputs.shape
    chans = target.shape[-1]
    axes = ("col", "ens")
    owners = lax.axis_size("col") * lax.axis_size("ens")
    each = cols // owners
    shards = lax.axis_size("col") * lax.axis_size("spread")
    gain = layer_norm_gain.reshape(1, width)
    lanes = members * width
    move = lambda g: lax.all_to_all(g, axes, split_axis=0, concat_axis=0, tiled=True)
    high = lax.reduce_precision(target, 8, 7)
    target_part = jnp.where(lax.axis_index("ens") == 0, high, target - high).astype(bf16)

    def outgoing(start, count):
        span = slice(start * owners, (start + count) * owners)
        send_x = inputs[:, :, span].reshape(members, lat, count, owners, width)
        send_x = send_x.transpose(3, 2, 1, 0, 4).reshape(owners, count, lat, lanes)
        send_t = target_part[:, span].reshape(lat, count, owners, chans).transpose(2, 1, 0, 3)
        return jnp.concatenate([send_x, send_t], axis=-1)

    lead = each // 2
    tail = each - lead
    x_lead = move(outgoing(0, lead))
    x_tail = move(outgoing(lead, tail))
    weights = (gain, w_qkv, w_out, w_head)
    g_lead, acc = block_call(x_lead, *weights, None, 0)
    g_lead = move(g_lead)
    g_tail, *sums = block_call(x_tail, *weights, acc, shards)
    g_tail = move(g_tail)
    share, g_lead, g_tail = reduce_rows((sums[:2], sums[2:]), g_lead, g_tail)
    share = share.astype(f32)
    columns = (
        lambda g: g.reshape(owners, -1, lat, members, width)
        .transpose(3, 2, 1, 0, 4)
        .reshape(members, lat, -1, width)
    )
    ready = columns(g_lead)
    ready = jnp.pad(ready, ((0, 0), (0, 0), (0, tail * owners), (0, 0)))
    ready = lax.optimization_barrier(ready)
    grad_input = lax.dynamic_update_slice(
        ready, columns(g_tail), (0, 0, lead * owners, 0)
    )
    grad_qkv = share[:, : 3 * width]
    grad_out = share[:, 3 * width : 4 * width]
    grad_head = share[:, 4 * width :]
    return (grad_input, grad_qkv, grad_out, grad_head)


def solution(mesh):
    groups, lon, ens = mesh.devices.shape
    split = Mesh(
        mesh.devices.reshape(groups, CELLS, lon // CELLS, ens), ("groups", "col", "spread", "ens")
    )
    lon_axes = ("col", "spread")
    in_specs = (
        P("ens", "groups", lon_axes, None),
        P(),
        P(),
        P(),
        P(),
        P("groups", lon_axes, None),
    )
    rows = P(("groups",) + lon_axes, None)
    out_specs = (P("ens", "groups", lon_axes, None), rows, rows, rows)
    return jax.shard_map(body, mesh=split, in_specs=in_specs, out_specs=out_specs, check_vma=False)
```

```python
import functools

import jax
import jax.numpy as jnp
from jax import lax
from jax.experimental import pallas as pl
from jax.experimental.pallas import tpu as pltpu
from jax.sharding import Mesh
from jax.sharding import PartitionSpec as P

HEADS = 16
CELLS = 8
eps_norm = 1e-05
smooth_width = 0.25
loss_scale = 32.0
LOG2E = 1.4426950408889634
LATE = 3

bf16 = jnp.bfloat16
f32 = jnp.float32


def dot(left, right):
    return jnp.dot(left, right, preferred_element_type=f32)


def dot_t(left, right):
    return lax.dot_general(left, right, (((1,), (1,)), ((), ())), preferred_element_type=f32)


def dot_rows(left, right):
    return lax.dot_general(left, right, (((0,), (0,)), ((), ())), preferred_element_type=f32)


def slope(delta):
    return delta * lax.rsqrt(delta * delta + smooth_width * smooth_width)


def expand(block, mask):
    return jnp.concatenate([block] * 4, axis=0) * mask


def diagonal(wide, lane, dim):
    cells = wide.shape[0] // 4
    out = wide[:cells]
    for h in range(1, 4):
        out = jnp.where(lane >= h * dim, wide[h * cells : (h + 1) * cells], out)
    return out


def block_kernel(members, width, chans, first, last, *refs):
    x_ref, gain_ref, wqkv_hbm, wout_hbm, whead_hbm = refs[:5]
    refs = refs[5:]
    if not first:
        prev_ref, refs = refs[0], refs[1:]
    gx_ref, refs = refs[0], refs[1:]
    if last:
        sum_refs, refs = refs[:4], refs[4:]
    else:
        acc_ref, refs = refs[0], refs[1:]
    xf, normed, normed_t, qkv, g_qkv, att, probs, bout, g_pred, g_block, g_att, mask_ref, acc = (
        refs[:13]
    )
    wqkv_ref, wout_ref, whead_ref, sems = refs[13:]
    fetches = [
        pltpu.make_async_copy(wqkv_hbm, wqkv_ref, sems.at[0]),
        pltpu.make_async_copy(wout_hbm, wout_ref, sems.at[1]),
        pltpu.make_async_copy(whead_hbm, whead_ref, sems.at[2]),
    ]
    if not first:
        fetches.append(pltpu.make_async_copy(prev_ref, acc, sems.at[3]))
    cells = CELLS * CELLS
    rows = members * cells
    half = members // 2
    dim = width // HEADS
    pack = 4 * dim
    packs = width // pack
    scale = dim ** (-0.5)
    step = pl.program_id(0)
    tile = 256

    @pl.when(step == 0)
    def _():
        for fetch in fetches:
            fetch.start()
        if first:
            acc[...] = jnp.zeros_like(acc)
        row_head = lax.broadcasted_iota(jnp.int32, (4 * cells, pack), 0) // cells
        lane_head = lax.broadcasted_iota(jnp.int32, (4 * cells, pack), 1) // dim
        mask_ref[...] = jnp.where(row_head == lane_head, 1.0, 0.0).astype(bf16)

    lane = lax.broadcasted_iota(jnp.int32, (cells, pack), 1)

    for c in range(CELLS):
        for s in range(2):
            for m in range(half):
                top = (s * half + m) * cells + c * CELLS
                xf[top : top + CELLS, :] = x_ref[
                    c * 2 + s, 0, :, m * width : (m + 1) * width
                ].astype(f32)

    gain = gain_ref[...]

    @pl.loop(0, members, unroll=True)
    def _(m):
        at = pl.ds(pl.multiple_of(m * cells, cells), cells)
        x = xf[at, :]
        centered = x - jnp.mean(x, axis=-1, keepdims=True)
        var = jnp.mean(centered * centered, axis=-1, keepdims=True)
        normed[at, :] = (centered * lax.rsqrt(var + eps_norm) * gain).astype(bf16)

    @pl.when(step == 0)
    def _():
        fetches[0].wait()

    @pl.loop(0, 3 * width // tile, unroll=True)
    def _(n):
        at = pl.ds(pl.multiple_of(n * tile, tile), tile)
        qkv[:, at] = dot(normed[...], wqkv_ref[:, at]).astype(bf16)

    @pl.loop(0, members, unroll=8)
    def _(m):
        at = pl.ds(pl.multiple_of(m * cells, cells), cells)
        mask = mask_ref[...]
        each = range(packs)
        part = lambda p, i: qkv[at, i * width + p * pack : i * width + (p + 1) * pack]
        scores = [dot_t(part(p, 1), expand(part(p, 0), mask)) for p in each]
        expos = [
            jnp.exp2((s - jnp.max(s, axis=0, keepdims=True)) * (scale * LOG2E)) for s in scores
        ]
        weights = [e * (1.0 / jnp.sum(e, axis=0, keepdims=True)) for e in expos]
        for p in each:
            probs[m, p] = weights[p]
        outs = [dot_rows(weights[p].astype(bf16), part(p, 2)) for p in each]
        for p in each:
            att[at, p * pack : (p + 1) * pack] = diagonal(outs[p], lane, dim).astype(bf16)

    @pl.when(step == 0)
    def _():
        for fetch in fetches[1:]:
            fetch.wait()

    bout[...] = (xf[...] + dot(att[...], wout_ref[...])).astype(bf16)
    pred = dot(bout[...], whead_ref[...]).astype(bf16).astype(f32).reshape(members, cells, chans)
    parts = []
    for c in range(CELLS):
        high = x_ref[c * 2, 0, :, half * width :].astype(f32)
        low = x_ref[c * 2 + 1, 0, :, half * width :].astype(f32)
        parts.append(high + low)
    target = jnp.concatenate(parts, axis=0)
    pair = [jnp.zeros((cells, chans), f32) for _ in range(members)]
    for a in range(members):
        for b in range(a + 1, members):
            s = slope(pred[a] - pred[b])
            pair[a] = pair[a] + s
            pair[b] = pair[b] - s
    for a in range(members):
        g_pred[a * cells : (a + 1) * cells, :] = (
            loss_scale / members * (slope(pred[a] - target) - pair[a] / (members - 1))
        ).astype(bf16)
    g_block[...] = dot_t(g_pred[...], whead_ref[...]).astype(bf16)
    g_att[...] = dot_t(g_block[...], wout_ref[...]).astype(bf16)

    @pl.loop(0, members, unroll=8)
    def _(m):
        at = pl.ds(pl.multiple_of(m * cells, cells), cells)
        mask = mask_ref[...]
        each = range(packs)
        part = lambda p, i: qkv[at, i * width + p * pack : i * width + (p + 1) * pack]
        ups = [expand(g_att[at, p * pack : (p + 1) * pack], mask) for p in each]
        g_probs = [dot_t(part(p, 2), ups[p]) for p in each]
        g_vs = [dot(probs[m, p].astype(bf16), ups[p]) for p in each]
        g_scores = []
        for p in each:
            prob = probs[m, p]
            inner = jnp.sum(prob * g_probs[p], axis=0, keepdims=True)
            g_scores.append((prob * (g_probs[p] - inner) * scale).astype(bf16))
        g_qs = [dot_rows(g_scores[p], part(p, 1)) for p in each]
        g_ks = [dot(g_scores[p], expand(part(p, 0), mask)) for p in each]
        for p in each:
            at_p = lambda i: pl.ds(i * width + p * pack, pack)
            g_qkv[at, at_p(0)] = diagonal(g_qs[p], lane, dim).astype(bf16)
            g_qkv[at, at_p(1)] = g_ks[p].astype(bf16)
            g_qkv[at, at_p(2)] = g_vs[p].astype(bf16)

    normed_t[...] = normed[...].T

    @pl.loop(0, 3 * width // tile, unroll=True)
    def _(n):
        at = pl.ds(pl.multiple_of(n * tile, tile), tile)
        acc[:, at] += dot(normed_t[...], g_qkv[:, at])

    normed_t[...] = att[...].T

    @pl.loop(0, width // tile, unroll=True)
    def _(n):
        at = pl.ds(pl.multiple_of(n * tile, tile), tile)
        there = pl.ds(pl.multiple_of(3 * width + n * tile, tile), tile)
        acc[:, there] += dot(normed_t[...], g_block[:, at])

    acc[:, 4 * width :] += dot_rows(bout[...], g_pred[...])

    @pl.when(step == pl.num_programs(0) - 1)
    def _():
        if last:
            core = lax.axis_index("ens")
            shards, piece, cut = sum_refs[0].shape
            for b in range(shards):
                for i, span in enumerate((slice(0, cut), slice(cut, acc.shape[1]))):
                    low = acc[2 * b * piece : (2 * b + 1) * piece, span]
                    high = acc[(2 * b + 1) * piece : (2 * b + 2) * piece, span]
                    sum_refs[2 * i][b] = jnp.where(core == 0, low, high).astype(bf16)
                    sum_refs[2 * i + 1][b] = jnp.where(core == 0, high, low).astype(bf16)
        else:
            pltpu.make_async_copy(acc, acc_ref, sems.at[3]).start()

    @pl.loop(0, width // tile, unroll=True)
    def _(n):
        at = pl.ds(pl.multiple_of(n * tile, tile), tile)
        g_att[:, at] = dot_t(g_qkv[...], wqkv_ref[at, :]).astype(bf16)

    for m in range(members):
        x = xf[m * cells : (m + 1) * cells, :]
        centered = x - jnp.mean(x, axis=-1, keepdims=True)
        var = jnp.mean(centered * centered, axis=-1, keepdims=True)
        rstd = lax.rsqrt(var + eps_norm)
        xhat = centered * rstd
        h = g_att[m * cells : (m + 1) * cells, :].astype(f32) * gain
        grad = rstd * (
            h
            - jnp.mean(h, axis=-1, keepdims=True)
            - xhat * jnp.mean(h * xhat, axis=-1, keepdims=True)
        )
        grad = grad + g_block[m * cells : (m + 1) * cells, :].astype(f32)
        s, mm = m // half, m % half
        for c in range(CELLS):
            gx_ref[c * 2 + s, 0, :, mm * width : (mm + 1) * width] = grad[
                c * CELLS : (c + 1) * CELLS, :
            ].astype(bf16)

    if not last:

        @pl.when(step == pl.num_programs(0) - 1)
        def _():
            pltpu.make_async_copy(acc, acc_ref, sems.at[3]).wait()


def block_call(x, gain, w_qkv, w_out, w_head, prev, shards):
    sources, count, lat = x.shape[:3]
    width, chans = w_head.shape
    members = 8
    lanes = members // 2 * width
    rows = members * CELLS * CELLS
    total = 4 * width + chans
    whole = lambda shape: pl.BlockSpec(shape, lambda i: (0,) * len(shape))
    anywhere = pl.BlockSpec(memory_space=pl.ANY)
    in_specs = [
        pl.BlockSpec((sources, 1, lat, lanes + chans), lambda i: (0, i, 0, 0)),
        whole((1, width)),
        anywhere,
        anywhere,
        anywhere,
    ]
    args = [x, gain, w_qkv, w_out, w_head]
    if prev is not None:
        in_specs.append(anywhere)
        args.append(prev)
    cells = CELLS * CELLS
    pack = 4 * (width // HEADS)
    out_specs = [pl.BlockSpec((sources, 1, lat, lanes), lambda i: (0, i, 0, 0))]
    out_shape = [jax.ShapeDtypeStruct((sources, count, lat, lanes), bf16)]
    if shards:
        cut = total // 256 * 128
        for part in (cut, cut, total - cut, total - cut):
            sums = (shards, width // shards // 2, part)
            out_specs.append(whole(sums))
            out_shape.append(jax.ShapeDtypeStruct(sums, bf16))
    else:
        out_specs.append(anywhere)
        out_shape.append(jax.ShapeDtypeStruct((width, total), f32))
    return pl.pallas_call(
        functools.partial(block_kernel, members, width, chans, prev is None, shards > 0),
        grid=(count,),
        in_specs=in_specs,
        out_specs=out_specs,
        out_shape=out_shape,
        scratch_shapes=[
            pltpu.VMEM((rows, width), f32),
            pltpu.VMEM((rows, width), bf16),
            pltpu.VMEM((rows, width), bf16),
            pltpu.VMEM((rows, 3 * width), bf16),
            pltpu.VMEM((rows, 3 * width), bf16),
            pltpu.VMEM((rows, width), bf16),
            pltpu.VMEM((members, width // pack, cells, 4 * cells), f32),
            pltpu.VMEM((rows, width), bf16),
            pltpu.VMEM((rows, chans), bf16),
            pltpu.VMEM((rows, width), bf16),
            pltpu.VMEM((rows, width), bf16),
            pltpu.VMEM((4 * cells, pack), bf16),
            pltpu.VMEM((width, total), f32),
            pltpu.VMEM(w_qkv.shape, bf16),
            pltpu.VMEM(w_out.shape, bf16),
            pltpu.VMEM(w_head.shape, bf16),
            pltpu.SemaphoreType.DMA((4,)),
        ],
        compiler_params=pltpu.CompilerParams(vmem_limit_bytes=60 * 1024 * 1024),
        cost_estimate=pl.CostEstimate(
            flops=count * 8_000_000_000, bytes_accessed=16_000_000, transcendentals=1_000_000
        ),
        name="grid_block",
    )(*args)


def swap_sum(kept, given, axes, bit):
    count = 1
    for axis in axes:
        count *= lax.axis_size(axis)
    taken = lax.ppermute(given, axes, [(i, i ^ bit) for i in range(count)])
    return (kept.astype(f32) + taken.astype(f32)).astype(kept.dtype)


def reduce_rows(sums, early, late):
    lon = ("col", "spread")
    shards = lax.axis_size("col") * lax.axis_size("spread")
    bits = shards.bit_length() - 1
    assert shards == 1 << bits
    me = lax.axis_index(lon)
    first = lax.axis_index("ens") == 0
    (*sums, early) = lax.optimization_barrier((*sums, early))
    rest = [swap_sum(mine, given, ("ens",), 1) for mine, given in sums]
    rest = [r.reshape((2,) * bits + r.shape[1:]) for r in rest]
    orders = [list(range(bits))] * 2
    left = [list(range(bits))[::-1] for _ in orders]
    for i in range(bits):
        if i == LATE:
            *rest, late = lax.optimization_barrier((*rest, late))
        for c, order in enumerate(orders):
            axis = left[c].index(order[i])
            left[c].remove(order[i])
            low, high = (lax.index_in_dim(rest[c], h, axis, keepdims=False) for h in range(2))
            mine = (me >> order[i]) % 2 == 0
            rest[c] = swap_sum(
                jnp.where(mine, low, high), jnp.where(mine, high, low), lon, 1 << order[i]
            )
    if LATE >= bits:
        *rest, late = lax.optimization_barrier((*rest, late))
    share = jnp.concatenate(rest, axis=-1)
    other = lax.ppermute(share, "ens", [(0, 1), (1, 0)])
    share = jnp.concatenate(
        [jnp.where(first, share, other), jnp.where(first, other, share)], axis=0
    )
    return share, early, late


def body(inputs, layer_norm_gain, w_qkv, w_out, w_head, target):
    members, lat, cols, width = inputs.shape
    chans = target.shape[-1]
    axes = ("col", "ens")
    owners = lax.axis_size("col") * lax.axis_size("ens")
    each = cols // owners
    shards = lax.axis_size("col") * lax.axis_size("spread")
    gain = layer_norm_gain.reshape(1, width)
    lanes = members * width
    move = lambda g: lax.all_to_all(g, axes, split_axis=0, concat_axis=0, tiled=True)
    high = lax.reduce_precision(target, 8, 7)
    target_part = jnp.where(lax.axis_index("ens") == 0, high, target - high).astype(bf16)

    def outgoing(start, count):
        span = slice(start * owners, (start + count) * owners)
        send_x = inputs[:, :, span].reshape(members, lat, count, owners, width)
        send_x = send_x.transpose(3, 2, 1, 0, 4).reshape(owners, count, lat, lanes)
        send_t = target_part[:, span].reshape(lat, count, owners, chans).transpose(2, 1, 0, 3)
        return jnp.concatenate([send_x, send_t], axis=-1)

    lead = each // 2
    tail = each - lead
    x_lead = move(outgoing(0, lead))
    x_tail = move(outgoing(lead, tail))
    weights = (gain, w_qkv, w_out, w_head)
    g_lead, acc = block_call(x_lead, *weights, None, 0)
    g_lead = move(g_lead)
    g_tail, *sums = block_call(x_tail, *weights, acc, shards)
    g_tail = move(g_tail)
    share, g_lead, g_tail = reduce_rows((sums[:2], sums[2:]), g_lead, g_tail)
    share = share.astype(f32)
    columns = (
        lambda g: g.reshape(owners, -1, lat, members, width)
        .transpose(3, 2, 1, 0, 4)
        .reshape(members, lat, -1, width)
    )
    ready = columns(g_lead)
    ready = jnp.pad(ready, ((0, 0), (0, 0), (0, tail * owners), (0, 0)))
    ready = lax.optimization_barrier(ready)
    grad_input = lax.dynamic_update_slice(
        ready, columns(g_tail), (0, 0, lead * owners, 0)
    )
    grad_qkv = share[:, : 3 * width]
    grad_out = share[:, 3 * width : 4 * width]
    grad_head = share[:, 4 * width :]
    return (grad_input, grad_qkv, grad_out, grad_head)


def solution(mesh):
    groups, lon, ens = mesh.devices.shape
    split = Mesh(
        mesh.devices.reshape(groups, CELLS, lon // CELLS, ens), ("groups", "col", "spread", "ens")
    )
    lon_axes = ("col", "spread")
    in_specs = (
        P("ens", "groups", lon_axes, None),
        P(),
        P(),
        P(),
        P(),
        P("groups", lon_axes, None),
    )
    rows = P(("groups",) + lon_axes, None)
    out_specs = (P("ens", "groups", lon_axes, None), rows, rows, rows)
    return jax.shard_map(body, mesh=split, in_specs=in_specs, out_specs=out_specs, check_vma=False)
```
